512 devices in a mesh: node: 128 (over y, z_hi, x), slab: 4 (over z_lo, core).
Axes of the slice: x: 4, y: 8, z: 8 (z_hi: 4, z_lo: 2; z = z_hi * 2 + z_lo), core: 2. Of those that a mesh axis runs over, the one named last changes fastest.
Arguments:
- points: float32 [65536, 64], P(('node', 'slab')), may hold values from -6 to 6
- probes: float32 [65536, 128], P(('node', 'slab')), may hold values from -1.5 to 1.5
- leaf: int32 [65536, 1], P(('node', 'slab')), may hold values from 0 to 127; in each aligned block of 128 rows (0 to 127, 128 to 255, ...) at most 4 rows name the same one
Outputs:
- sketches: float32 [65536, 128], P(('node', 'slab'))
The draws below stay inside these ranges and needn't reach their ends.
Inputs may be any that keep to these rules, and one draw needn't show every extreme that they name: `leaf`: among the 128 points of one device, at most 4 name any one cluster, and exactly 4 name some cluster on some device.
All inputs are finite; a program needn't handle non-finite values.
Results may differ from the reference program's by a relative error of at most 0.00008.
Values sent between devices are 32-bit elements; how exact they have to be, the bound alone decides.
No kernel may reach another device: no remote copies, remote signals or barrier semaphores. Data moves between devices by JAX's collectives and lax.ppermute only.
A program may use at most 64 MiB of HBM per device.

```python
import math
import jax
import jax.numpy as jnp
import numpy as np
from jax import lax

D = 64
R = 64
PTS_DEV = 128
CLUSTERS = 128
CAP = 4
POINTS = 65536
N_NODE = 128
N_SLAB = 4


def steps_of(stream_key, extent, shards, low, top_value):
    level = 1.0
    for position, parts in shards:
        steps = jax.random.uniform(jax.random.fold_in(jax.random.fold_in(stream_key, 6), position), (parts,), jnp.float32, low / len(shards), top_value / len(shards))
        level = level * jnp.repeat(jnp.exp(steps), extent[position] // parts).reshape((-1,) + (1,) * (len(extent) - 1 - position))
    return level


def assign_block(own_key, own, number, rows, amount, top, limit, lean):
    sequence = jax.random.permutation(own_key, amount)
    packed, common = shares(amount, rows * top, limit, lean, True), shares(amount, rows * top, limit, lean, False)
    places = jnp.arange(amount)

    def named(lengths, offset_by):
        used = int((lengths > 0).sum())
        fixed = max(1, used // 4)
        passed = fixed + (places - fixed + offset_by * (used - fixed)) % max(1, amount - fixed)
        return jnp.zeros((amount,), jnp.int32).at[sequence[jnp.where(places < fixed, places, passed)]].set(jnp.asarray(lengths, jnp.int32))

    lengths = jnp.where(number % 4 == 0, named(packed, number // 4), named(common, number - number // 4 - 1))
    mixed = jax.random.permutation(jax.random.fold_in(own, 3), amount)
    source_of, taker = mixed[0:amount // 2 * 2:2], mixed[1:amount // 2 * 2:2]
    room = jnp.minimum(lengths[source_of] - 1, limit - lengths[taker]) // 2
    room = jnp.where((source_of == sequence[0]) | (taker == sequence[0]) | (lengths[taker] == 0), 0, jnp.maximum(room, 0))
    passed = jax.random.randint(jax.random.fold_in(own, 4), (amount // 2,), 0, 1 << 20) % (room + 1)
    lengths = lengths.at[source_of].add(-passed).at[taker].add(passed)
    members = jnp.searchsorted(jnp.cumsum(lengths), jnp.arange(rows * top), side="right").astype(jnp.int32)
    grid = members.reshape(top, rows).T
    grid = grid[jax.random.permutation(jax.random.fold_in(own, 1), rows)]
    offset_by = jax.random.randint(jax.random.fold_in(own, 2), (rows, 1), 0, top)
    return jnp.take_along_axis(grid, (jnp.arange(top)[None, :] + offset_by) % top, axis=1)


def shares(count, total, limit, lean, full):
    loads = [(1 << 20) // math.isqrt(grade ** lean) + 1 for grade in range(1, count + 1)]
    largest = limit if full else min(limit, max(-(-total // count), total * loads[0] // sum(loads)))
    least = 1 if total - largest >= count - 1 else 0
    counts, spare = [largest] + [least] * (count - 1), total - largest - least * (count - 1)
    while spare > 0:
        candidates = [i for i in range(1, count) if counts[i] < largest] or [i for i in range(1, count) if counts[i] < limit]
        mass, left = sum([loads[i] for i in candidates]), spare
        for i in candidates:
            addition = min(limit - counts[i], max(1, left * loads[i] // mass), spare)
            counts[i] = counts[i] + addition
            spare = spare - addition
    return np.array(counts)


def gaussian(stream_key, dims, scale, bound, cuts=(), kind=jnp.bfloat16):
    factor_of = steps_of(stream_key, dims, cuts, -0.22, 0.18) if cuts else 1.0
    result = jax.random.normal(stream_key, dims, jnp.float32) * scale * factor_of
    return jnp.minimum(jnp.maximum(result, -bound), bound).astype(kind)


def setup_inputs(seed: int = 0) -> dict:
    key_list = jax.random.split(jax.random.key(seed), 4)
    points = gaussian(key_list[0], (POINTS, D), 1.0, 6.0, ((0, 512),), jnp.float32)
    probes = gaussian(key_list[1], (POINTS, 2 * R), 0.25, 1.5, ((0, 512),), jnp.float32)
    leaf_keys = jax.random.split(jax.random.fold_in(key_list[2], 1), POINTS // PTS_DEV)
    leaf_turns = jax.random.permutation(jax.random.fold_in(key_list[2], 3), POINTS // PTS_DEV)
    leaf = jax.vmap(lambda own, number: assign_block(jax.random.fold_in(key_list[2], 2), own, number, PTS_DEV, CLUSTERS, 1, CAP, 2))(leaf_keys, leaf_turns).reshape((POINTS, 1))
    return dict(points=points, probes=probes, leaf=leaf)


kernel_scale = 1.0 / 64.0


def kernel_apply(own_x, cols):
    col_x = cols[:, :D]
    col_w = cols[:, D:]
    cross = jnp.dot(own_x, col_x.T, precision=lax.Precision.HIGHEST, preferred_element_type=jnp.float32)
    dist = jnp.sum(own_x * own_x, axis=1)[:, None] + jnp.sum(col_x * col_x, axis=1)[None, :] - 2.0 * cross
    weights = jnp.exp(-kernel_scale * dist)
    return jnp.dot(weights, col_w, precision=lax.Precision.HIGHEST, preferred_element_type=jnp.float32)


def reference(points, probes, leaf):
    n_dev = N_NODE * N_SLAB
    cap = 4 * PTS_DEV // N_NODE
    slots = N_NODE * cap
    dest = leaf[:, 0].reshape(n_dev, PTS_DEV)
    onehot = (dest[:, :, None] == jnp.arange(N_NODE, dtype=jnp.int32)[None, None, :]).astype(jnp.int32)
    before = jnp.cumsum(onehot, axis=1).astype(jnp.int32) - onehot
    slot = jnp.sum(before * onehot, axis=2).astype(jnp.int32)
    payload = jnp.concatenate([points, probes], axis=1)
    width = payload.shape[1]
    device_ids = jnp.arange(n_dev, dtype=jnp.int32)
    node_of = (device_ids // N_SLAB)[:, None]
    slab_of = (device_ids % N_SLAB)[:, None]
    place = ((slab_of * N_NODE + dest) * slots + node_of * cap + slot).reshape(-1).astype(jnp.int32)
    buffer = jnp.zeros((N_SLAB * N_NODE * slots, width), jnp.float32).at[place].set(payload)
    buffer = buffer.reshape(N_SLAB, N_NODE, slots, width)

    def one_cluster(cluster):
        own = lax.dynamic_index_in_dim(buffer, cluster, 1, keepdims=False).reshape(N_SLAB * slots, width)
        other = lax.dynamic_index_in_dim(buffer, jnp.bitwise_xor(cluster, 1), 1, keepdims=False).reshape(N_SLAB * slots, width)
        return kernel_apply(own[:, :D], other)

    results = lax.map(one_cluster, jnp.arange(N_NODE, dtype=jnp.int32))
    results = results.reshape(N_NODE * N_SLAB * slots, 2 * R)
    fetch = ((dest * N_SLAB + slab_of) * slots + node_of * cap + slot).reshape(-1).astype(jnp.int32)
    return results[fetch]
```

```python
import functools
import math

import jax
import jax.numpy as jnp
from jax import lax
from jax.experimental import pallas as pl
from jax.experimental.pallas import tpu as pltpu
from jax.sharding import PartitionSpec as P

kernel_scale = 1.0 / 64.0
log2_scale = kernel_scale * math.log2(math.e)
CAP = 4
UNIT = 6
LANES = 128


def split2(value):
    high = value.astype(jnp.bfloat16)
    low = (value - high.astype(jnp.float32)).astype(jnp.bfloat16)
    return high, low


def split3(value):
    high = value.astype(jnp.bfloat16)
    rest = value - high.astype(jnp.float32)
    mid = rest.astype(jnp.bfloat16)
    low = (rest - mid.astype(jnp.float32)).astype(jnp.bfloat16)
    return high, mid, low


def iota(shape, dim):
    return lax.broadcasted_iota(jnp.int32, shape, dim)


def nt(a, b):
    return lax.dot_general(a, b, (((1,), (1,)), ((), ())), preferred_element_type=jnp.float32)


def nn(a, b):
    return jnp.dot(a, b, preferred_element_type=jnp.float32)


def mask_bf16(mask):
    return jnp.where(mask, 1.0, 0.0).astype(jnp.bfloat16)


def pack_kernel(leaf_ref, xt_ref, w_ref, out_ref, pos_ref):
    n = leaf_ref.shape[1]
    dim = xt_ref.shape[0]
    leaf = leaf_ref[...]
    row = iota((LANES, n), 0)
    lane = iota((LANES, n), 1)
    own = row == leaf
    before = nn(mask_bf16(own), mask_bf16(row < lane))
    slot = jnp.sum(jnp.where(own, before, 0.0), axis=0, keepdims=True).astype(jnp.int32)
    pos_ref[...] = leaf * CAP + slot
    goal = jnp.bitwise_xor(leaf, 1) * CAP + slot
    choose = [mask_bf16(row * CAP == goal - j) for j in range(CAP)]
    w_parts = jnp.concatenate(split3(w_ref[...]), axis=1)
    for j in range(CAP):
        picked = nn(choose[j], w_parts)
        out_ref[pl.ds(j, LANES, stride=UNIT), :] = (
            picked[:, :LANES] + picked[:, LANES : 2 * LANES] + picked[:, 2 * LANES :]
        )
    empty = jnp.zeros((dim, n), jnp.bfloat16)
    x_parts = []
    for part in split3(xt_ref[...]):
        x_parts.append(jnp.concatenate([part, empty], axis=1))
        x_parts.append(jnp.concatenate([empty, part], axis=1))
    x_parts = jnp.concatenate(x_parts, axis=0)
    for h in range(CAP // 2):
        picked = nt(jnp.concatenate([choose[2 * h], choose[2 * h + 1]], axis=1), x_parts)
        out_ref[pl.ds(CAP + h, LANES, stride=UNIT), :] = (
            picked[:, :LANES] + picked[:, LANES : 2 * LANES] + picked[:, 2 * LANES :]
        )


def doubled(pair):
    turned = pltpu.roll(pair, 64, 1)
    low = iota(pair.shape, 1) < 64
    return jnp.concatenate([jnp.where(low, pair, turned), jnp.where(low, turned, pair)], axis=0)


def square_parts(x):
    total = jnp.sum(x * x, axis=1, keepdims=True) * (-0.5 * log2_scale)
    return [part.astype(jnp.float32) for part in split3(jnp.broadcast_to(total, x.shape))]


def left_operand(pair):
    x = doubled(pair)
    lane = iota(x.shape, 1)
    low = lane < 64
    s1, s2, s3 = square_parts(x)
    a1, a2, a3 = [part.astype(jnp.float32) for part in split3(x * (2.0 * log2_scale))]
    tail = jnp.where(lane < 3, 1.0, jnp.where(lane == 3, s1, jnp.where(lane == 4, s2, jnp.where(lane == 5, s3, 0.0))))
    parts = [a1, jnp.where(low, a2, a1), jnp.where(low, a3, a2), tail]
    return jnp.concatenate([part.astype(jnp.bfloat16) for part in parts], axis=1)


def right_operand(pair):
    x = doubled(pair)
    lane = iota(x.shape, 1)
    low = lane < 64
    s1, s2, s3 = square_parts(x)
    x1, x2, x3 = [part.astype(jnp.float32) for part in split3(x)]
    tail = jnp.where(lane == 0, s1, jnp.where(lane == 1, s2, jnp.where(lane == 2, s3, jnp.where(lane < 6, 1.0, 0.0))))
    first = jnp.where(low, x1, x2).astype(jnp.bfloat16)
    parts = [first, jnp.where(low, x1, x3).astype(jnp.bfloat16), first, tail.astype(jnp.bfloat16)]
    return jnp.concatenate(parts, axis=1)


def block_kernel(*refs, first, last):
    refs = list(refs)
    if first:
        own_ref = refs.pop(0)
    else:
        left_in, total_in = refs.pop(0), refs.pop(0)
    cols_ref = refs.pop(0)
    rows = LANES
    rights, values = [], []
    for h in range(CAP // 2):
        rights.append(right_operand(cols_ref[pl.ds(CAP + h, rows, stride=UNIT), :]))
        w = jnp.concatenate([cols_ref[pl.ds(2 * h + e, rows, stride=UNIT), :] for e in range(2)], axis=0)
        values.append(jnp.concatenate(split2(w), axis=1))
    if first:
        left_ref, total_ref = refs
        for h in range(CAP // 2):
            left_ref[pl.ds(2 * h * rows, 2 * rows), :] = left_operand(own_ref[pl.ds(h * rows, rows), :])
        source = left_ref
    else:
        (total_ref,) = refs
        source = left_in
    for j in range(CAP):
        left = source[pl.ds(j * rows, rows), :]
        total = None
        for h in range(CAP // 2):
            weights = jnp.exp2(nt(left, rights[h]))
            w1, w2 = split2(weights)
            part = nn(w1, values[h]) + nn(w2, values[h])
            total = part if total is None else total + part
        total = total[:, :LANES] + total[:, LANES:]
        if not first:
            total = total + total_in[pl.ds(j * rows, rows), :]
        if last:
            total_ref[pl.ds(j, rows, stride=CAP), :] = total
        else:
            total_ref[pl.ds(j * rows, rows), :] = total


def take_kernel(pos_ref, back_ref, out_ref):
    n = pos_ref.shape[1]
    slots = back_ref.shape[0]
    wanted = jnp.transpose(jnp.broadcast_to(pos_ref[...].astype(jnp.float32), (LANES, n))).astype(jnp.int32)
    lane = iota((n, LANES), 1)
    choose = jnp.concatenate([mask_bf16(wanted == lane + k * LANES) for k in range(slots // LANES)], axis=1)
    picked = nn(choose, jnp.concatenate(split3(back_ref[...]), axis=1))
    out_ref[...] = picked[:, :LANES] + picked[:, LANES : 2 * LANES] + picked[:, 2 * LANES :]


def coords_kernel(here_ref, out_ref):
    for h in range(CAP // 2):
        out_ref[pl.ds(h * LANES, LANES), :] = here_ref[pl.ds(CAP + h, LANES, stride=UNIT), :]


def whole(count):
    return [pl.BlockSpec(memory_space=pltpu.VMEM)] * count


def call(kernel, args, outs, flops):
    single = len(outs) == 1
    return pl.pallas_call(
        kernel,
        out_shape=outs[0] if single else outs,
        in_specs=whole(len(args)),
        out_specs=whole(1)[0] if single else whole(len(outs)),
        compiler_params=pltpu.CompilerParams(vmem_limit_bytes=24 * 1024 * 1024),
        cost_estimate=pl.CostEstimate(flops=flops, bytes_accessed=1 << 20, transcendentals=1 << 18),
    )(*args)


def swapped(value, axis, mask):
    pairs = [(source, source ^ mask) for source in range(lax.axis_size(axis))]
    return lax.ppermute(value, axis, pairs)


def per_device(points, probes, leaf):
    n_node = lax.axis_size("node")
    f32 = jnp.float32
    slots = n_node * CAP
    packed, pos = call(
        pack_kernel,
        (leaf.reshape(1, -1), points.T, probes),
        (jax.ShapeDtypeStruct((n_node * UNIT, LANES), f32), jax.ShapeDtypeStruct((1, leaf.shape[0]), jnp.int32)),
        1 << 28,
    )
    arrived = lax.all_to_all(
        packed.reshape(n_node, 1, UNIT * LANES), "node", split_axis=0, concat_axis=0, tiled=True
    )
    here = arrived.reshape(n_node * UNIT, LANES)
    far = swapped(here, "slab", 2)
    coords = call(coords_kernel, (here,), (jax.ShapeDtypeStruct((2 * n_node, LANES), f32),), 1 << 10)
    own = swapped(coords, "node", 1)
    beside = swapped(here, "slab", 1)
    total_shape = jax.ShapeDtypeStruct((slots, LANES), f32)
    flops = 1 << 31
    left, total = call(
        functools.partial(block_kernel, first=True, last=False),
        (own, here),
        (jax.ShapeDtypeStruct((slots, 4 * LANES), jnp.bfloat16), total_shape),
        flops,
    )
    middle = functools.partial(block_kernel, first=False, last=False)
    total = call(middle, (left, total, beside), (total_shape,), flops)
    far, total = lax.optimization_barrier((far, total))
    far_beside = swapped(far, "slab", 1)
    total = call(middle, (left, total, far), (total_shape,), flops)
    total = call(
        functools.partial(block_kernel, first=False, last=True), (left, total, far_beside), (total_shape,), flops
    )
    back = lax.all_to_all(
        total.reshape(n_node, CAP, LANES), "node", split_axis=0, concat_axis=0, tiled=True
    ).reshape(slots, LANES)
    return call(take_kernel, (pos, back), (jax.ShapeDtypeStruct(probes.shape, f32),), 1 << 27)


def solution(mesh):
    placed = (P(("node", "slab"), None), P(("node", "slab"), None), P(("node", "slab"), None))
    return jax.shard_map(
        per_device, mesh=mesh, in_specs=placed, out_specs=P(("node", "slab"), None), check_vma=False
    )
```

```python
import functools
import math

import jax
import jax.numpy as jnp
from jax import lax
from jax.experimental import pallas as pl
from jax.experimental.pallas import tpu as pltpu
from jax.sharding import PartitionSpec as P

kernel_scale = 1.0 / 64.0
log2_scale = kernel_scale * math.log2(math.e)
CAP = 4
UNIT = 6
LANES = 128


def split2(value):
    high = value.astype(jnp.bfloat16)
    low = (value - high.astype(jnp.float32)).astype(jnp.bfloat16)
    return high, low


def split3(value):
    high = value.astype(jnp.bfloat16)
    rest = value - high.astype(jnp.float32)
    mid = rest.astype(jnp.bfloat16)
    low = (rest - mid.astype(jnp.float32)).astype(jnp.bfloat16)
    return high, mid, low


def iota(shape, dim):
    return lax.broadcasted_iota(jnp.int32, shape, dim)


def nt(a, b):
    return lax.dot_general(a, b, (((1,), (1,)), ((), ())), preferred_element_type=jnp.float32)


def nn(a, b):
    return jnp.dot(a, b, preferred_element_type=jnp.float32)


def mask_bf16(mask):
    return jnp.where(mask, 1.0, 0.0).astype(jnp.bfloat16)


def choose_kernel(pos_ref, choose_ref):
    n = pos_ref.shape[1]
    wanted = jnp.transpose(jnp.broadcast_to(pos_ref[...].astype(jnp.float32), (LANES, n))).astype(jnp.int32)
    lane = iota((n, LANES), 1)
    for k in range(choose_ref.shape[1] // LANES):
        choose_ref[:, k * LANES : (k + 1) * LANES] = mask_bf16(wanted == lane + k * LANES)


def earlier_kernel(out_ref):
    out_ref[...] = mask_bf16(iota(out_ref.shape, 0) < iota(out_ref.shape, 1))


def pack_kernel(earlier_ref, leaf_ref, xt_ref, w_ref, out_ref, pos_ref):
    n = leaf_ref.shape[1]
    dim = xt_ref.shape[0]
    leaf = leaf_ref[...]
    row = iota((LANES, n), 0)
    own = row == leaf
    before = nn(mask_bf16(own), earlier_ref[...])
    slot = jnp.sum(jnp.where(own, before, 0.0), axis=0, keepdims=True).astype(jnp.int32)
    pos_ref[...] = leaf * CAP + slot
    goal = jnp.bitwise_xor(leaf, 1) * CAP + slot
    choose = [mask_bf16(row * CAP == goal - j) for j in range(CAP)]
    w_parts = jnp.concatenate(split3(w_ref[...]), axis=1)
    for j in range(CAP):
        picked = nn(choose[j], w_parts)
        out_ref[pl.ds(j, LANES, stride=UNIT), :] = (
            picked[:, :LANES] + picked[:, LANES : 2 * LANES] + picked[:, 2 * LANES :]
        )
    empty = jnp.zeros((dim, n), jnp.bfloat16)
    x_parts = []
    for part in split3(xt_ref[...]):
        x_parts.append(jnp.concatenate([part, empty], axis=1))
        x_parts.append(jnp.concatenate([empty, part], axis=1))
    x_parts = jnp.concatenate(x_parts, axis=0)
    for h in range(CAP // 2):
        picked = nt(jnp.concatenate([choose[2 * h], choose[2 * h + 1]], axis=1), x_parts)
        out_ref[pl.ds(CAP + h, LANES, stride=UNIT), :] = (
            picked[:, :LANES] + picked[:, LANES : 2 * LANES] + picked[:, 2 * LANES :]
        )


def doubled(pair):
    turned = pltpu.roll(pair, 64, 1)
    low = iota(pair.shape, 1) < 64
    return jnp.concatenate([jnp.where(low, pair, turned), jnp.where(low, turned, pair)], axis=0)


def square_parts(x):
    total = jnp.sum(x * x, axis=1, keepdims=True) * (-0.5 * log2_scale)
    return [part.astype(jnp.float32) for part in split3(jnp.broadcast_to(total, x.shape))]


def left_operand(pair):
    x = doubled(pair)
    lane = iota(x.shape, 1)
    low = lane < 64
    s1, s2, s3 = square_parts(x)
    a1, a2, a3 = [part.astype(jnp.float32) for part in split3(x * (2.0 * log2_scale))]
    tail = jnp.where(lane < 3, 1.0, jnp.where(lane == 3, s1, jnp.where(lane == 4, s2, jnp.where(lane == 5, s3, 0.0))))
    parts = [a1, jnp.where(low, a2, a1), jnp.where(low, a3, a2), tail]
    return jnp.concatenate([part.astype(jnp.bfloat16) for part in parts], axis=1)


def right_operand(pair):
    x = doubled(pair)
    lane = iota(x.shape, 1)
    low = lane < 64
    s1, s2, s3 = square_parts(x)
    x1, x2, x3 = [part.astype(jnp.float32) for part in split3(x)]
    tail = jnp.where(lane == 0, s1, jnp.where(lane == 1, s2, jnp.where(lane == 2, s3, jnp.where(lane < 6, 1.0, 0.0))))
    first = jnp.where(low, x1, x2).astype(jnp.bfloat16)
    parts = [first, jnp.where(low, x1, x3).astype(jnp.bfloat16), first, tail.astype(jnp.bfloat16)]
    return jnp.concatenate(parts, axis=1)


def block_kernel(*refs, first, last):
    refs = list(refs)
    if first:
        own_ref = refs.pop(0)
    else:
        left_in, total_in = refs.pop(0), refs.pop(0)
    cols_ref = refs.pop(0)
    rows = LANES
    rights, values = [], []
    for h in range(CAP // 2):
        rights.append(right_operand(cols_ref[pl.ds(CAP + h, rows, stride=UNIT), :]))
        w = jnp.concatenate([cols_ref[pl.ds(2 * h + e, rows, stride=UNIT), :] for e in range(2)], axis=0)
        values.append(jnp.concatenate(split2(w), axis=1))
    if first:
        left_ref, total_ref = refs
        for h in range(CAP // 2):
            left_ref[pl.ds(2 * h * rows, 2 * rows), :] = left_operand(own_ref[pl.ds(h * rows, rows), :])
        source = left_ref
    else:
        (total_ref,) = refs
        source = left_in
    left = source[...]
    total = None
    for h in range(CAP // 2):
        w1, w2 = split2(jnp.exp2(nt(left, rights[h])))
        part = nn(w1, values[h]) + nn(w2, values[h])
        total = part if total is None else total + part
    total = total[:, :LANES] + total[:, LANES:]
    if not first:
        total = total + total_in[...]
    if last:
        for j in range(CAP):
            total_ref[pl.ds(j, rows, stride=CAP), :] = total[j * rows : (j + 1) * rows, :]
    else:
        total_ref[...] = total


def take_kernel(choose_ref, back_ref, out_ref):
    picked = nn(choose_ref[...], jnp.concatenate(split3(back_ref[...]), axis=1))
    out_ref[...] = picked[:, :LANES] + picked[:, LANES : 2 * LANES] + picked[:, 2 * LANES :]


def coords_kernel(here_ref, out_ref):
    for h in range(CAP // 2):
        out_ref[pl.ds(h * LANES, LANES), :] = here_ref[pl.ds(CAP + h, LANES, stride=UNIT), :]


def whole(count):
    return [pl.BlockSpec(memory_space=pltpu.VMEM)] * count


def call(kernel, args, outs, flops):
    single = len(outs) == 1
    return pl.pallas_call(
        kernel,
        out_shape=outs[0] if single else outs,
        in_specs=whole(len(args)),
        out_specs=whole(1)[0] if single else whole(len(outs)),
        compiler_params=pltpu.CompilerParams(vmem_limit_bytes=24 * 1024 * 1024),
        cost_estimate=pl.CostEstimate(flops=flops, bytes_accessed=1 << 10, transcendentals=0),
    )(*args)


def swapped(value, axis, mask):
    pairs = [(source, source ^ mask) for source in range(lax.axis_size(axis))]
    return lax.ppermute(value, axis, pairs)


def per_device(points, probes, leaf):
    n_node = lax.axis_size("node")
    f32 = jnp.float32
    slots = n_node * CAP
    bf16 = jnp.bfloat16
    earlier = call(earlier_kernel, (), (jax.ShapeDtypeStruct((LANES, leaf.shape[0]), bf16),), 1 << 33)
    packed, pos = call(
        pack_kernel,
        (earlier, leaf.reshape(1, -1), points.T, probes),
        (jax.ShapeDtypeStruct((n_node * UNIT, LANES), f32), jax.ShapeDtypeStruct((1, leaf.shape[0]), jnp.int32)),
        1 << 28,
    )
    arrived = lax.all_to_all(
        packed.reshape(n_node, 1, UNIT * LANES), "node", split_axis=0, concat_axis=0, tiled=True
    )
    here = arrived.reshape(n_node * UNIT, LANES)
    far = swapped(here, "slab", 2)
    coords = call(coords_kernel, (here,), (jax.ShapeDtypeStruct((2 * n_node, LANES), f32),), 1 << 10)
    own = swapped(coords, "node", 1)
    beside = swapped(here, "slab", 1)
    total_shape = jax.ShapeDtypeStruct((slots, LANES), f32)
    flops = 1 << 12
    left, total = call(
        functools.partial(block_kernel, first=True, last=False),
        (own, here),
        (jax.ShapeDtypeStruct((slots, 4 * LANES), jnp.bfloat16), total_shape),
        flops,
    )
    middle = functools.partial(block_kernel, first=False, last=False)
    choose = call(choose_kernel, (pos,), (jax.ShapeDtypeStruct((leaf.shape[0], slots), bf16),), 1 << 12)
    far, total, choose = lax.optimization_barrier((far, total, choose))
    far_beside = swapped(far, "slab", 1)
    total = call(middle, (left, total, far), (total_shape,), flops)
    total = call(middle, (left, total, beside), (total_shape,), flops)
    total = call(
        functools.partial(block_kernel, first=False, last=True), (left, total, far_beside), (total_shape,), flops
    )
    back = lax.all_to_all(
        total.reshape(n_node, CAP, LANES), "node", split_axis=0, concat_axis=0, tiled=True
    ).reshape(slots, LANES)
    return call(take_kernel, (choose, back), (jax.ShapeDtypeStruct(probes.shape, f32),), 1 << 27)


def solution(mesh):
    placed = (P(("node", "slab"), None), P(("node", "slab"), None), P(("node", "slab"), None))
    return jax.shard_map(
        per_device, mesh=mesh, in_specs=placed, out_specs=P(("node", "slab"), None), check_vma=False
    )
```

```python
import functools
import math

import jax
import jax.numpy as jnp
from jax import lax
from jax.experimental import pallas as pl
from jax.experimental.pallas import tpu as pltpu
from jax.sharding import PartitionSpec as P

kernel_scale = 1.0 / 64.0
log2_scale = kernel_scale * math.log2(math.e)
CAP = 4
UNIT = 6
LANES = 128
NODE_Y, NODE_Z, NODE_X = 8, 4, 4


def split2(value):
    high = value.astype(jnp.bfloat16)
    low = (value - high.astype(jnp.float32)).astype(jnp.bfloat16)
    return high, low


def split3(value):
    high = value.astype(jnp.bfloat16)
    rest = value - high.astype(jnp.float32)
    mid = rest.astype(jnp.bfloat16)
    low = (rest - mid.astype(jnp.float32)).astype(jnp.bfloat16)
    return high, mid, low


def iota(shape, dim):
    return lax.broadcasted_iota(jnp.int32, shape, dim)


def nt(a, b):
    return lax.dot_general(a, b, (((1,), (1,)), ((), ())), preferred_element_type=jnp.float32)


def nn(a, b):
    return jnp.dot(a, b, preferred_element_type=jnp.float32)


def mask_bf16(mask):
    return jnp.where(mask, 1.0, 0.0).astype(jnp.bfloat16)


def choose_kernel(pos_ref, choose_ref):
    n = pos_ref.shape[1]
    wanted = jnp.transpose(jnp.broadcast_to(pos_ref[...].astype(jnp.float32), (LANES, n))).astype(jnp.int32)
    lane = iota((n, LANES), 1)
    for k in range(choose_ref.shape[1] // LANES):
        choose_ref[:, k * LANES : (k + 1) * LANES] = mask_bf16(wanted == lane + k * LANES)


def earlier_kernel(out_ref):
    out_ref[...] = mask_bf16(iota(out_ref.shape, 0) < iota(out_ref.shape, 1))


def place(node):
    x = jnp.bitwise_and(node, NODE_X - 1)
    z = jnp.bitwise_and(node // NODE_X, NODE_Z - 1)
    return (x * NODE_Z + z) * NODE_Y + node // (NODE_X * NODE_Z)


def pack_kernel(earlier_ref, leaf_ref, xt_ref, w_ref, out_ref, pos_ref):
    n = leaf_ref.shape[1]
    dim = xt_ref.shape[0]
    leaf = leaf_ref[...]
    row = iota((LANES, n), 0)
    own = row == leaf
    before = nn(mask_bf16(own), earlier_ref[...])
    slot = jnp.sum(jnp.where(own, before, 0.0), axis=0, keepdims=True).astype(jnp.int32)
    pos_ref[...] = place(leaf) * CAP + slot
    goal = place(jnp.bitwise_xor(leaf, 1)) * CAP + slot
    choose = [mask_bf16(row * CAP == goal - j) for j in range(CAP)]
    w_parts = jnp.concatenate(split3(w_ref[...]), axis=1)
    for j in range(CAP):
        picked = nn(choose[j], w_parts)
        out_ref[pl.ds(j, LANES, stride=UNIT), :] = (
            picked[:, :LANES] + picked[:, LANES : 2 * LANES] + picked[:, 2 * LANES :]
        )
    empty = jnp.zeros((dim, n), jnp.bfloat16)
    x_parts = []
    for part in split3(xt_ref[...]):
        x_parts.append(jnp.concatenate([part, empty], axis=1))
        x_parts.append(jnp.concatenate([empty, part], axis=1))
    x_parts = jnp.concatenate(x_parts, axis=0)
    for h in range(CAP // 2):
        picked = nt(jnp.concatenate([choose[2 * h], choose[2 * h + 1]], axis=1), x_parts)
        out_ref[pl.ds(CAP + h, LANES, stride=UNIT), :] = (
            picked[:, :LANES] + picked[:, LANES : 2 * LANES] + picked[:, 2 * LANES :]
        )


def doubled(pair):
    turned = pltpu.roll(pair, 64, 1)
    low = iota(pair.shape, 1) < 64
    return jnp.concatenate([jnp.where(low, pair, turned), jnp.where(low, turned, pair)], axis=0)


def square_parts(x):
    total = jnp.sum(x * x, axis=1, keepdims=True) * (-0.5 * log2_scale)
    return [part.astype(jnp.float32) for part in split3(jnp.broadcast_to(total, x.shape))]


def left_operand(pair):
    x = doubled(pair)
    lane = iota(x.shape, 1)
    low = lane < 64
    s1, s2, s3 = square_parts(x)
    a1, a2, a3 = [part.astype(jnp.float32) for part in split3(x * (2.0 * log2_scale))]
    tail = jnp.where(lane < 3, 1.0, jnp.where(lane == 3, s1, jnp.where(lane == 4, s2, jnp.where(lane == 5, s3, 0.0))))
    parts = [a1, jnp.where(low, a2, a1), jnp.where(low, a3, a2), tail]
    return jnp.concatenate([part.astype(jnp.bfloat16) for part in parts], axis=1)


def right_operand(pair):
    x = doubled(pair)
    lane = iota(x.shape, 1)
    low = lane < 64
    s1, s2, s3 = square_parts(x)
    x1, x2, x3 = [part.astype(jnp.float32) for part in split3(x)]
    tail = jnp.where(lane == 0, s1, jnp.where(lane == 1, s2, jnp.where(lane == 2, s3, jnp.where(lane < 6, 1.0, 0.0))))
    first = jnp.where(low, x1, x2).astype(jnp.bfloat16)
    parts = [first, jnp.where(low, x1, x3).astype(jnp.bfloat16), first, tail.astype(jnp.bfloat16)]
    return jnp.concatenate(parts, axis=1)


def block_kernel(*refs, first, last):
    refs = list(refs)
    if first:
        own_ref = refs.pop(0)
    else:
        left_in, total_in = refs.pop(0), refs.pop(0)
    cols_ref = refs.pop(0)
    rows = LANES
    rights, values = [], []
    for h in range(CAP // 2):
        rights.append(right_operand(cols_ref[pl.ds(CAP + h, rows, stride=UNIT), :]))
        w = jnp.concatenate([cols_ref[pl.ds(2 * h + e, rows, stride=UNIT), :] for e in range(2)], axis=0)
        values.append(jnp.concatenate(split2(w), axis=1))
    if first:
        left_ref, total_ref = refs
        for h in range(CAP // 2):
            left_ref[pl.ds(2 * h * rows, 2 * rows), :] = left_operand(own_ref[pl.ds(h * rows, rows), :])
        source = left_ref
    else:
        (total_ref,) = refs
        source = left_in
    left = source[...]
    main, rest = 0.0, 0.0
    for h in range(CAP // 2):
        w1, w2 = split2(jnp.exp2(nt(left, rights[h])))
        main = main + nn(w1, values[h])
        rest = rest + nn(w2, values[h][:, :LANES])
    total = main[:, :LANES] + (main[:, LANES:] + rest)
    if not first:
        total = total + total_in[...]
    if last:
        for j in range(CAP):
            total_ref[pl.ds(j, rows, stride=CAP), :] = total[j * rows : (j + 1) * rows, :]
    else:
        total_ref[...] = total


def take_kernel(choose_ref, back_ref, out_ref):
    picked = nn(choose_ref[...], jnp.concatenate(split3(back_ref[...]), axis=1))
    out_ref[...] = picked[:, :LANES] + picked[:, LANES : 2 * LANES] + picked[:, 2 * LANES :]


def coords_kernel(here_ref, out_ref):
    for h in range(CAP // 2):
        out_ref[pl.ds(h * LANES, LANES), :] = here_ref[pl.ds(CAP + h, LANES, stride=UNIT), :]


def whole(count):
    return [pl.BlockSpec(memory_space=pltpu.VMEM)] * count


def call(kernel, args, outs, flops):
    single = len(outs) == 1
    return pl.pallas_call(
        kernel,
        out_shape=outs[0] if single else outs,
        in_specs=whole(len(args)),
        out_specs=whole(1)[0] if single else whole(len(outs)),
        compiler_params=pltpu.CompilerParams(vmem_limit_bytes=24 * 1024 * 1024),
        cost_estimate=pl.CostEstimate(flops=flops, bytes_accessed=1 << 10, transcendentals=0),
    )(*args)


def exchanged(value):
    order = [(y * NODE_Z + z) * NODE_X + x for x in range(NODE_X) for z in range(NODE_Z) for y in range(NODE_Y)]
    return lax.all_to_all(value, "node", split_axis=0, concat_axis=0, axis_index_groups=[order], tiled=True)


def swapped(value, axis, mask):
    pairs = [(source, source ^ mask) for source in range(lax.axis_size(axis))]
    return lax.ppermute(value, axis, pairs)


def per_device(points, probes, leaf):
    n_node = lax.axis_size("node")
    f32 = jnp.float32
    slots = n_node * CAP
    bf16 = jnp.bfloat16
    earlier = call(earlier_kernel, (), (jax.ShapeDtypeStruct((LANES, leaf.shape[0]), bf16),), 1 << 33)
    packed, pos = call(
        pack_kernel,
        (earlier, leaf.reshape(1, -1), points.T, probes),
        (jax.ShapeDtypeStruct((n_node * UNIT, LANES), f32), jax.ShapeDtypeStruct((1, leaf.shape[0]), jnp.int32)),
        1 << 28,
    )
    arrived = exchanged(packed.reshape(n_node, 1, UNIT * LANES))
    here = arrived.reshape(n_node * UNIT, LANES)
    far = swapped(here, "slab", 2)
    coords = call(coords_kernel, (here,), (jax.ShapeDtypeStruct((2 * n_node, LANES), f32),), 1 << 10)
    own = swapped(coords, "node", 1)
    beside = swapped(here, "slab", 1)
    total_shape = jax.ShapeDtypeStruct((slots, LANES), f32)
    flops = 1 << 12
    left, total = call(
        functools.partial(block_kernel, first=True, last=False),
        (own, here),
        (jax.ShapeDtypeStruct((slots, 4 * LANES), jnp.bfloat16), total_shape),
        flops,
    )
    middle = functools.partial(block_kernel, first=False, last=False)
    choose = call(choose_kernel, (pos,), (jax.ShapeDtypeStruct((leaf.shape[0], slots), bf16),), 1 << 12)
    far, total, choose = lax.optimization_barrier((far, total, choose))
    far_beside = swapped(far, "slab", 1)
    total = call(middle, (left, total, far), (total_shape,), flops)
    total = call(middle, (left, total, beside), (total_shape,), flops)
    total = call(
        functools.partial(block_kernel, first=False, last=True), (left, total, far_beside), (total_shape,), flops
    )
    back = exchanged(total.reshape(n_node, CAP, LANES)).reshape(slots, LANES)
    return call(take_kernel, (choose, back), (jax.ShapeDtypeStruct(probes.shape, f32),), 1 << 27)


def solution(mesh):
    placed = (P(("node", "slab"), None), P(("node", "slab"), None), P(("node", "slab"), None))
    return jax.shard_map(
        per_device, mesh=mesh, in_specs=placed, out_specs=P(("node", "slab"), None), check_vma=False
    )
```

```python
import functools
import math

import jax
import jax.numpy as jnp
from jax import lax
from jax.experimental import pallas as pl
from jax.experimental.pallas import tpu as pltpu
from jax.sharding import PartitionSpec as P

kernel_scale = 1.0 / 64.0
log2_scale = kernel_scale * math.log2(math.e)
CAP = 4
UNIT = 6
LANES = 128
NODE_Y, NODE_Z, NODE_X = 8, 4, 4


def split2(value):
    high = value.astype(jnp.bfloat16)
    low = (value - high.astype(jnp.float32)).astype(jnp.bfloat16)
    return high, low


def split3(value):
    high = value.astype(jnp.bfloat16)
    rest = value - high.astype(jnp.float32)
    mid = rest.astype(jnp.bfloat16)
    low = (rest - mid.astype(jnp.float32)).astype(jnp.bfloat16)
    return high, mid, low


def iota(shape, dim):
    return lax.broadcasted_iota(jnp.int32, shape, dim)


def nt(a, b):
    return lax.dot_general(a, b, (((1,), (1,)), ((), ())), preferred_element_type=jnp.float32)


def nn(a, b):
    return jnp.dot(a, b, preferred_element_type=jnp.float32)


def mask_bf16(mask):
    return jnp.where(mask, 1.0, 0.0).astype(jnp.bfloat16)


def choose_kernel(pos_ref, choose_ref):
    n = pos_ref.shape[1]
    wanted = jnp.transpose(jnp.broadcast_to(pos_ref[...].astype(jnp.float32), (LANES, n))).astype(jnp.int32)
    lane = iota((n, LANES), 1)
    for k in range(choose_ref.shape[1] // LANES):
        choose_ref[:, k * LANES : (k + 1) * LANES] = mask_bf16(wanted == lane + k * LANES)


def earlier_kernel(out_ref):
    out_ref[...] = mask_bf16(iota(out_ref.shape, 0) < iota(out_ref.shape, 1))


def place(node, odd):
    x = jnp.bitwise_and(node, NODE_X - 1)
    z = jnp.bitwise_and(node // NODE_X, NODE_Z - 1)
    rank = (x * NODE_Z + z) * NODE_Y + node // (NODE_X * NODE_Z)
    return jnp.where(odd, NODE_X * NODE_Y * NODE_Z - 1 - rank, rank)


def pack_kernel(earlier_ref, leaf_ref, xt_ref, w_ref, out_ref, pos_ref):
    n = leaf_ref.shape[1]
    dim = xt_ref.shape[0]
    leaf = leaf_ref[...]
    row = iota((LANES, n), 0)
    own = row == leaf
    before = nn(mask_bf16(own), earlier_ref[...])
    slot = jnp.sum(jnp.where(own, before, 0.0), axis=0, keepdims=True).astype(jnp.int32)
    odd = lax.axis_index("slab") % 2 == 1
    pos_ref[...] = place(leaf, odd) * CAP + slot
    goal = place(jnp.bitwise_xor(leaf, 1), odd) * CAP + slot
    choose = [mask_bf16(row * CAP == goal - j) for j in range(CAP)]
    w_parts = jnp.concatenate(split3(w_ref[...]), axis=1)
    for j in range(CAP):
        picked = nn(choose[j], w_parts)
        out_ref[pl.ds(j, LANES, stride=UNIT), :] = (
            picked[:, :LANES] + picked[:, LANES : 2 * LANES] + picked[:, 2 * LANES :]
        )
    empty = jnp.zeros((dim, n), jnp.bfloat16)
    x_parts = []
    for part in split3(xt_ref[...]):
        x_parts.append(jnp.concatenate([part, empty], axis=1))
        x_parts.append(jnp.concatenate([empty, part], axis=1))
    x_parts = jnp.concatenate(x_parts, axis=0)
    for h in range(CAP // 2):
        picked = nt(jnp.concatenate([choose[2 * h], choose[2 * h + 1]], axis=1), x_parts)
        out_ref[pl.ds(CAP + h, LANES, stride=UNIT), :] = (
            picked[:, :LANES] + picked[:, LANES : 2 * LANES] + picked[:, 2 * LANES :]
        )


def doubled(pair):
    turned = pltpu.roll(pair, 64, 1)
    low = iota(pair.shape, 1) < 64
    return jnp.concatenate([jnp.where(low, pair, turned), jnp.where(low, turned, pair)], axis=0)


def square_parts(x):
    total = jnp.sum(x * x, axis=1, keepdims=True) * (-0.5 * log2_scale)
    return [part.astype(jnp.float32) for part in split3(jnp.broadcast_to(total, x.shape))]


def left_operand(pair):
    x = doubled(pair)
    lane = iota(x.shape, 1)
    low = lane < 64
    s1, s2, s3 = square_parts(x)
    a1, a2, a3 = [part.astype(jnp.float32) for part in split3(x * (2.0 * log2_scale))]
    tail = jnp.where(lane < 3, 1.0, jnp.where(lane == 3, s1, jnp.where(lane == 4, s2, jnp.where(lane == 5, s3, 0.0))))
    parts = [a1, jnp.where(low, a2, a1), jnp.where(low, a3, a2), tail]
    return jnp.concatenate([part.astype(jnp.bfloat16) for part in parts], axis=1)


def right_operand(pair):
    x = doubled(pair)
    lane = iota(x.shape, 1)
    low = lane < 64
    s1, s2, s3 = square_parts(x)
    x1, x2, x3 = [part.astype(jnp.float32) for part in split3(x)]
    tail = jnp.where(lane == 0, s1, jnp.where(lane == 1, s2, jnp.where(lane == 2, s3, jnp.where(lane < 6, 1.0, 0.0))))
    first = jnp.where(low, x1, x2).astype(jnp.bfloat16)
    parts = [first, jnp.where(low, x1, x3).astype(jnp.bfloat16), first, tail.astype(jnp.bfloat16)]
    return jnp.concatenate(parts, axis=1)


def block_kernel(*refs, first, last):
    refs = list(refs)
    if first:
        own_ref = refs.pop(0)
    else:
        left_in, total_in = refs.pop(0), refs.pop(0)
    cols_ref = refs.pop(0)
    rows = LANES
    rights, values = [], []
    for h in range(CAP // 2):
        rights.append(right_operand(cols_ref[pl.ds(CAP + h, rows, stride=UNIT), :]))
        w = jnp.concatenate([cols_ref[pl.ds(2 * h + e, rows, stride=UNIT), :] for e in range(2)], axis=0)
        values.append(jnp.concatenate(split2(w), axis=1))
    if first:
        left_ref, total_ref = refs
        for h in range(CAP // 2):
            left_ref[pl.ds(2 * h * rows, 2 * rows), :] = left_operand(own_ref[pl.ds(h * rows, rows), :])
        source = left_ref
    else:
        (total_ref,) = refs
        source = left_in
    left = source[...]
    main, rest = 0.0, 0.0
    for h in range(CAP // 2):
        w1, w2 = split2(jnp.exp2(nt(left, rights[h])))
        main = main + nn(w1, values[h])
        rest = rest + nn(w2, values[h][:, :LANES])
    total = main[:, :LANES] + (main[:, LANES:] + rest)
    if not first:
        total = total + total_in[...]
    if last:
        for j in range(CAP):
            total_ref[pl.ds(j, rows, stride=CAP), :] = total[j * rows : (j + 1) * rows, :]
    else:
        total_ref[...] = total


def take_kernel(choose_ref, back_ref, out_ref):
    picked = nn(choose_ref[...], jnp.concatenate(split3(back_ref[...]), axis=1))
    out_ref[...] = picked[:, :LANES] + picked[:, LANES : 2 * LANES] + picked[:, 2 * LANES :]


def coords_kernel(here_ref, out_ref):
    for h in range(CAP // 2):
        out_ref[pl.ds(h * LANES, LANES), :] = here_ref[pl.ds(CAP + h, LANES, stride=UNIT), :]


def whole(count):
    return [pl.BlockSpec(memory_space=pltpu.VMEM)] * count


def call(kernel, args, outs, flops):
    single = len(outs) == 1
    return pl.pallas_call(
        kernel,
        out_shape=outs[0] if single else outs,
        in_specs=whole(len(args)),
        out_specs=whole(1)[0] if single else whole(len(outs)),
        compiler_params=pltpu.CompilerParams(vmem_limit_bytes=24 * 1024 * 1024),
        cost_estimate=pl.CostEstimate(flops=flops, bytes_accessed=1 << 10, transcendentals=0),
    )(*args)


def exchanged(value):
    order = [(y * NODE_Z + z) * NODE_X + x for x in range(NODE_X) for z in range(NODE_Z) for y in range(NODE_Y)]
    n_slab = lax.axis_size("slab")
    groups = [[n * n_slab + s for n in (order if s % 2 == 0 else order[::-1])] for s in range(n_slab)]
    return lax.all_to_all(
        value, ("node", "slab"), split_axis=0, concat_axis=0, axis_index_groups=groups, tiled=True
    )


def swapped(value, axis, mask):
    pairs = [(source, source ^ mask) for source in range(lax.axis_size(axis))]
    return lax.ppermute(value, axis, pairs)


def per_device(points, probes, leaf):
    n_node = lax.axis_size("node")
    f32 = jnp.float32
    slots = n_node * CAP
    bf16 = jnp.bfloat16
    earlier = call(earlier_kernel, (), (jax.ShapeDtypeStruct((LANES, leaf.shape[0]), bf16),), 1 << 33)
    packed, pos = call(
        pack_kernel,
        (earlier, leaf.reshape(1, -1), points.T, probes),
        (jax.ShapeDtypeStruct((n_node * UNIT, LANES), f32), jax.ShapeDtypeStruct((1, leaf.shape[0]), jnp.int32)),
        1 << 28,
    )
    arrived = exchanged(packed.reshape(n_node, 1, UNIT * LANES))
    here = arrived.reshape(n_node * UNIT, LANES)
    far = swapped(here, "slab", 2)
    coords = call(coords_kernel, (here,), (jax.ShapeDtypeStruct((2 * n_node, LANES), f32),), 1 << 10)
    own = swapped(coords, "node", 1)
    beside = swapped(here, "slab", 1)
    total_shape = jax.ShapeDtypeStruct((slots, LANES), f32)
    flops = 1 << 12
    left, total = call(
        functools.partial(block_kernel, first=True, last=False),
        (own, here),
        (jax.ShapeDtypeStruct((slots, 4 * LANES), jnp.bfloat16), total_shape),
        flops,
    )
    middle = functools.partial(block_kernel, first=False, last=False)
    choose = call(choose_kernel, (pos,), (jax.ShapeDtypeStruct((leaf.shape[0], slots), bf16),), 1 << 12)
    far, total, choose = lax.optimization_barrier((far, total, choose))
    far_beside = swapped(far, "slab", 1)
    total = call(middle, (left, total, far), (total_shape,), flops)
    total = call(middle, (left, total, beside), (total_shape,), flops)
    total = call(
        functools.partial(block_kernel, first=False, last=True), (left, total, far_beside), (total_shape,), flops
    )
    back = exchanged(total.reshape(n_node, CAP, LANES)).reshape(slots, LANES)
    return call(take_kernel, (choose, back), (jax.ShapeDtypeStruct(probes.shape, f32),), 1 << 27)


def solution(mesh):
    placed = (P(("node", "slab"), None), P(("node", "slab"), None), P(("node", "slab"), None))
    return jax.shard_map(
        per_device, mesh=mesh, in_specs=placed, out_specs=P(("node", "slab"), None), check_vma=False
    )
```

```python
import functools
import math

import jax
import jax.numpy as jnp
from jax import lax
from jax.experimental import pallas as pl
from jax.experimental.pallas import tpu as pltpu
from jax.sharding import PartitionSpec as P

kernel_scale = 1.0 / 64.0
log2_scale = kernel_scale * math.log2(math.e)
CAP = 4
UNIT = 6
LANES = 128
NODE_Y, NODE_Z, NODE_X = 8, 4, 4


def split2(value):
    high = value.astype(jnp.bfloat16)
    low = (value - high.astype(jnp.float32)).astype(jnp.bfloat16)
    return high, low


def split3(value):
    high = value.astype(jnp.bfloat16)
    rest = value - high.astype(jnp.float32)
    mid = rest.astype(jnp.bfloat16)
    low = (rest - mid.astype(jnp.float32)).astype(jnp.bfloat16)
    return high, mid, low


def iota(shape, dim):
    return lax.broadcasted_iota(jnp.int32, shape, dim)


def nt(a, b):
    return lax.dot_general(a, b, (((1,), (1,)), ((), ())), preferred_element_type=jnp.float32)


def nn(a, b):
    return jnp.dot(a, b, preferred_element_type=jnp.float32)


def mask_bf16(mask):
    return jnp.where(mask, 1.0, 0.0).astype(jnp.bfloat16)


def choose_kernel(pos_ref, choose_ref):
    n = pos_ref.shape[1]
    wanted = jnp.transpose(jnp.broadcast_to(pos_ref[...].astype(jnp.float32), (LANES, n))).astype(jnp.int32)
    lane = iota((n, LANES), 1)
    for k in range(choose_ref.shape[1] // LANES):
        choose_ref[:, k * LANES : (k + 1) * LANES] = mask_bf16(wanted == lane + k * LANES)


def earlier_kernel(out_ref):
    out_ref[...] = mask_bf16(iota(out_ref.shape, 0) < iota(out_ref.shape, 1))


def place(node):
    x = jnp.bitwise_and(node, NODE_X - 1)
    z = jnp.bitwise_and(node // NODE_X, NODE_Z - 1)
    rank = (x * NODE_Z + z) * NODE_Y + node // (NODE_X * NODE_Z)
    return NODE_X * NODE_Y * NODE_Z - 1 - rank


def pack_kernel(earlier_ref, leaf_ref, xt_ref, w_ref, out_ref, pos_ref):
    n = leaf_ref.shape[1]
    dim = xt_ref.shape[0]
    leaf = leaf_ref[...]
    row = iota((LANES, n), 0)
    own = row == leaf
    before = nn(mask_bf16(own), earlier_ref[...])
    slot = jnp.sum(jnp.where(own, before, 0.0), axis=0, keepdims=True).astype(jnp.int32)
    pos_ref[...] = place(leaf) * CAP + slot
    goal = place(jnp.bitwise_xor(leaf, 1)) * CAP + slot
    choose = [mask_bf16(row * CAP == goal - j) for j in range(CAP)]
    w_parts = jnp.concatenate(split3(w_ref[...]), axis=1)
    for j in range(CAP):
        picked = nn(choose[j], w_parts)
        out_ref[pl.ds(j, LANES, stride=UNIT), :] = (
            picked[:, :LANES] + picked[:, LANES : 2 * LANES] + picked[:, 2 * LANES :]
        )
    empty = jnp.zeros((dim, n), jnp.bfloat16)
    x_parts = []
    for part in split3(xt_ref[...]):
        x_parts.append(jnp.concatenate([part, empty], axis=1))
        x_parts.append(jnp.concatenate([empty, part], axis=1))
    x_parts = jnp.concatenate(x_parts, axis=0)
    for h in range(CAP // 2):
        picked = nt(jnp.concatenate([choose[2 * h], choose[2 * h + 1]], axis=1), x_parts)
        out_ref[pl.ds(CAP + h, LANES, stride=UNIT), :] = (
            picked[:, :LANES] + picked[:, LANES : 2 * LANES] + picked[:, 2 * LANES :]
        )


def doubled(pair):
    turned = pltpu.roll(pair, 64, 1)
    low = iota(pair.shape, 1) < 64
    return jnp.concatenate([jnp.where(low, pair, turned), jnp.where(low, turned, pair)], axis=0)


def square_parts(x):
    total = jnp.sum(x * x, axis=1, keepdims=True) * (-0.5 * log2_scale)
    return [part.astype(jnp.float32) for part in split3(jnp.broadcast_to(total, x.shape))]


def left_operand(pair):
    x = doubled(pair)
    lane = iota(x.shape, 1)
    low = lane < 64
    s1, s2, s3 = square_parts(x)
    a1, a2, a3 = [part.astype(jnp.float32) for part in split3(x * (2.0 * log2_scale))]
    tail = jnp.where(lane < 3, 1.0, jnp.where(lane == 3, s1, jnp.where(lane == 4, s2, jnp.where(lane == 5, s3, 0.0))))
    parts = [a1, jnp.where(low, a2, a1), jnp.where(low, a3, a2), tail]
    return jnp.concatenate([part.astype(jnp.bfloat16) for part in parts], axis=1)


def right_operand(pair):
    x = doubled(pair)
    lane = iota(x.shape, 1)
    low = lane < 64
    s1, s2, s3 = square_parts(x)
    x1, x2, x3 = [part.astype(jnp.float32) for part in split3(x)]
    tail = jnp.where(lane == 0, s1, jnp.where(lane == 1, s2, jnp.where(lane == 2, s3, jnp.where(lane < 6, 1.0, 0.0))))
    first = jnp.where(low, x1, x2).astype(jnp.bfloat16)
    parts = [first, jnp.where(low, x1, x3).astype(jnp.bfloat16), first, tail.astype(jnp.bfloat16)]
    return jnp.concatenate(parts, axis=1)


def block_kernel(*refs, first, last):
    refs = list(refs)
    if first:
        own_ref = refs.pop(0)
    else:
        left_in, total_in = refs.pop(0), refs.pop(0)
    cols_ref = refs.pop(0)
    rows = LANES
    rights, values = [], []
    for h in range(CAP // 2):
        rights.append(right_operand(cols_ref[pl.ds(CAP + h, rows, stride=UNIT), :]))
        w = jnp.concatenate([cols_ref[pl.ds(2 * h + e, rows, stride=UNIT), :] for e in range(2)], axis=0)
        values.append(jnp.concatenate(split2(w), axis=1))
    if first:
        left_ref, total_ref = refs
        for h in range(CAP // 2):
            left_ref[pl.ds(2 * h * rows, 2 * rows), :] = left_operand(own_ref[pl.ds(h * rows, rows), :])
        source = left_ref
    else:
        (total_ref,) = refs
        source = left_in
    left = source[...]
    main, rest = 0.0, 0.0
    for h in range(CAP // 2):
        w1, w2 = split2(jnp.exp2(nt(left, rights[h])))
        main = main + nn(w1, values[h])
        rest = rest + nn(w2, values[h][:, :LANES])
    total = main[:, :LANES] + (main[:, LANES:] + rest)
    if not first:
        total = total + total_in[...]
    if last:
        for j in range(CAP):
            total_ref[pl.ds(j, rows, stride=CAP), :] = total[j * rows : (j + 1) * rows, :]
    else:
        total_ref[...] = total


def take_kernel(choose_ref, back_ref, out_ref):
    picked = nn(choose_ref[...], jnp.concatenate(split3(back_ref[...]), axis=1))
    out_ref[...] = picked[:, :LANES] + picked[:, LANES : 2 * LANES] + picked[:, 2 * LANES :]


def coords_kernel(here_ref, out_ref):
    for h in range(CAP // 2):
        out_ref[pl.ds(h * LANES, LANES), :] = here_ref[pl.ds(CAP + h, LANES, stride=UNIT), :]


def whole(count):
    return [pl.BlockSpec(memory_space=pltpu.VMEM)] * count


def call(kernel, args, outs, flops):
    single = len(outs) == 1
    return pl.pallas_call(
        kernel,
        out_shape=outs[0] if single else outs,
        in_specs=whole(len(args)),
        out_specs=whole(1)[0] if single else whole(len(outs)),
        compiler_params=pltpu.CompilerParams(vmem_limit_bytes=24 * 1024 * 1024),
        cost_estimate=pl.CostEstimate(flops=flops, bytes_accessed=1 << 10, transcendentals=0),
    )(*args)


def exchanged(value):
    order = [(y * NODE_Z + z) * NODE_X + x for x in range(NODE_X) for z in range(NODE_Z) for y in range(NODE_Y)]
    return lax.all_to_all(value, "node", split_axis=0, concat_axis=0, axis_index_groups=[order[::-1]], tiled=True)


def swapped(value, axis, mask):
    pairs = [(source, source ^ mask) for source in range(lax.axis_size(axis))]
    return lax.ppermute(value, axis, pairs)


def per_device(points, probes, leaf):
    n_node = lax.axis_size("node")
    f32 = jnp.float32
    slots = n_node * CAP
    bf16 = jnp.bfloat16
    earlier = call(earlier_kernel, (), (jax.ShapeDtypeStruct((LANES, leaf.shape[0]), bf16),), 1 << 33)
    packed, pos = call(
        pack_kernel,
        (earlier, leaf.reshape(1, -1), points.T, probes),
        (jax.ShapeDtypeStruct((n_node * UNIT, LANES), f32), jax.ShapeDtypeStruct((1, leaf.shape[0]), jnp.int32)),
        1 << 28,
    )
    arrived = exchanged(packed.reshape(n_node, 1, UNIT * LANES))
    here = arrived.reshape(n_node * UNIT, LANES)
    far = swapped(here, "slab", 2)
    coords = call(coords_kernel, (here,), (jax.ShapeDtypeStruct((2 * n_node, LANES), f32),), 1 << 10)
    own = swapped(coords, "node", 1)
    beside = swapped(here, "slab", 1)
    total_shape = jax.ShapeDtypeStruct((slots, LANES), f32)
    flops = 1 << 12
    left, total = call(
        functools.partial(block_kernel, first=True, last=False),
        (own, here),
        (jax.ShapeDtypeStruct((slots, 4 * LANES), jnp.bfloat16), total_shape),
        flops,
    )
    middle = functools.partial(block_kernel, first=False, last=False)
    choose = call(choose_kernel, (pos,), (jax.ShapeDtypeStruct((leaf.shape[0], slots), bf16),), 1 << 12)
    far, total, choose = lax.optimization_barrier((far, total, choose))
    far_beside = swapped(far, "slab", 1)
    total = call(middle, (left, total, far), (total_shape,), flops)
    total = call(middle, (left, total, beside), (total_shape,), flops)
    total = call(
        functools.partial(block_kernel, first=False, last=True), (left, total, far_beside), (total_shape,), flops
    )
    back = exchanged(total.reshape(n_node, CAP, LANES)).reshape(slots, LANES)
    return call(take_kernel, (choose, back), (jax.ShapeDtypeStruct(probes.shape, f32),), 1 << 27)


def solution(mesh):
    placed = (P(("node", "slab"), None), P(("node", "slab"), None), P(("node", "slab"), None))
    return jax.shard_map(
        per_device, mesh=mesh, in_specs=placed, out_specs=P(("node", "slab"), None), check_vma=False
    )
```

```python
import functools
import math

import jax
import jax.numpy as jnp
from jax import lax
from jax.experimental import pallas as pl
from jax.experimental.pallas import tpu as pltpu
from jax.sharding import PartitionSpec as P

kernel_scale = 1.0 / 64.0
log2_scale = kernel_scale * math.log2(math.e)
CAP = 4
UNIT = 6
LANES = 128
NODE_Y, NODE_Z, NODE_X = 8, 4, 4


def split2(value):
    high = value.astype(jnp.bfloat16)
    low = (value - high.astype(jnp.float32)).astype(jnp.bfloat16)
    return high, low


def split3(value):
    high = value.astype(jnp.bfloat16)
    rest = value - high.astype(jnp.float32)
    mid = rest.astype(jnp.bfloat16)
    low = (rest - mid.astype(jnp.float32)).astype(jnp.bfloat16)
    return high, mid, low


def iota(shape, dim):
    return lax.broadcasted_iota(jnp.int32, shape, dim)


def nt(a, b):
    return lax.dot_general(a, b, (((1,), (1,)), ((), ())), preferred_element_type=jnp.float32)


def nn(a, b):
    return jnp.dot(a, b, preferred_element_type=jnp.float32)


def mask_bf16(mask):
    return jnp.where(mask, 1.0, 0.0).astype(jnp.bfloat16)


def choose_kernel(pos_ref, choose_ref):
    n = pos_ref.shape[1]
    wanted = jnp.transpose(jnp.broadcast_to(pos_ref[...].astype(jnp.float32), (LANES, n))).astype(jnp.int32)
    lane = iota((n, LANES), 1)
    for k in range(choose_ref.shape[1] // LANES):
        choose_ref[:, k * LANES : (k + 1) * LANES] = mask_bf16(wanted == lane + k * LANES)


def earlier_kernel(out_ref):
    out_ref[...] = mask_bf16(iota(out_ref.shape, 0) < iota(out_ref.shape, 1))


def place(node):
    x = jnp.bitwise_and(node, NODE_X - 1)
    z = jnp.bitwise_and(node // NODE_X, NODE_Z - 1)
    rank = (z * NODE_X + jnp.bitwise_xor(x, x // 2)) * NODE_Y + node // (NODE_X * NODE_Z)
    return NODE_X * NODE_Y * NODE_Z - 1 - rank


def pack_kernel(earlier_ref, leaf_ref, xt_ref, w_ref, out_ref, pos_ref):
    n = leaf_ref.shape[1]
    dim = xt_ref.shape[0]
    leaf = leaf_ref[...]
    row = iota((LANES, n), 0)
    own = row == leaf
    before = nn(mask_bf16(own), earlier_ref[...])
    slot = jnp.sum(jnp.where(own, before, 0.0), axis=0, keepdims=True).astype(jnp.int32)
    pos_ref[...] = place(leaf) * CAP + slot
    goal = place(jnp.bitwise_xor(leaf, 1)) * CAP + slot
    choose = [mask_bf16(row * CAP == goal - j) for j in range(CAP)]
    picked = nn(jnp.concatenate(choose, axis=0), jnp.concatenate(split3(w_ref[...]), axis=1))
    picked = picked[:, :LANES] + picked[:, LANES : 2 * LANES] + picked[:, 2 * LANES :]
    for j in range(CAP):
        out_ref[pl.ds(j, LANES, stride=UNIT), :] = picked[j * LANES : (j + 1) * LANES, :]
    empty = jnp.zeros((dim, n), jnp.bfloat16)
    x_parts = []
    for part in split3(xt_ref[...]):
        x_parts.append(jnp.concatenate([part, empty], axis=1))
        x_parts.append(jnp.concatenate([empty, part], axis=1))
    pairs = [jnp.concatenate(choose[2 * h : 2 * h + 2], axis=1) for h in range(CAP // 2)]
    picked = nt(jnp.concatenate(pairs, axis=0), jnp.concatenate(x_parts, axis=0))
    picked = picked[:, :LANES] + picked[:, LANES : 2 * LANES] + picked[:, 2 * LANES :]
    for h in range(CAP // 2):
        out_ref[pl.ds(CAP + h, LANES, stride=UNIT), :] = picked[h * LANES : (h + 1) * LANES, :]


def doubled(pair):
    turned = pltpu.roll(pair, 64, 1)
    low = iota(pair.shape, 1) < 64
    return jnp.concatenate([jnp.where(low, pair, turned), jnp.where(low, turned, pair)], axis=0)


def square_parts(x):
    total = jnp.sum(x * x, axis=1, keepdims=True) * (-0.5 * log2_scale)
    return [part.astype(jnp.float32) for part in split3(jnp.broadcast_to(total, x.shape))]


def left_operand(pair):
    x = doubled(pair)
    lane = iota(x.shape, 1)
    low = lane < 64
    s1, s2, s3 = square_parts(x)
    a1, a2, a3 = [part.astype(jnp.float32) for part in split3(x * (2.0 * log2_scale))]
    tail = jnp.where(lane < 3, 1.0, jnp.where(lane == 3, s1, jnp.where(lane == 4, s2, jnp.where(lane == 5, s3, 0.0))))
    parts = [a1, jnp.where(low, a2, a1), jnp.where(low, a3, a2), tail]
    return jnp.concatenate([part.astype(jnp.bfloat16) for part in parts], axis=1)


def right_operand(pair):
    x = doubled(pair)
    lane = iota(x.shape, 1)
    low = lane < 64
    s1, s2, s3 = square_parts(x)
    x1, x2, x3 = [part.astype(jnp.float32) for part in split3(x)]
    tail = jnp.where(lane == 0, s1, jnp.where(lane == 1, s2, jnp.where(lane == 2, s3, jnp.where(lane < 6, 1.0, 0.0))))
    first = jnp.where(low, x1, x2).astype(jnp.bfloat16)
    parts = [first, jnp.where(low, x1, x3).astype(jnp.bfloat16), first, tail.astype(jnp.bfloat16)]
    return jnp.concatenate(parts, axis=1)


def block_kernel(*refs, blocks, first, last):
    refs = list(refs)
    if first:
        own_ref = refs.pop(0)
    else:
        left_in, total_in = refs.pop(0), refs.pop(0)
    cols_refs, refs = refs[:blocks], refs[blocks:]
    rows = LANES
    if first:
        left_ref, total_ref = refs
        for h in range(CAP // 2):
            left_ref[pl.ds(2 * h * rows, 2 * rows), :] = left_operand(own_ref[pl.ds(h * rows, rows), :])
        source = left_ref
    else:
        (total_ref,) = refs
        source = left_in
    left = source[...]
    main, rest = 0.0, 0.0
    for cols_ref in cols_refs:
        for h in range(CAP // 2):
            right = right_operand(cols_ref[pl.ds(CAP + h, rows, stride=UNIT), :])
            w = jnp.concatenate([cols_ref[pl.ds(2 * h + e, rows, stride=UNIT), :] for e in range(2)], axis=0)
            high, low = split2(w)
            w1, w2 = split2(jnp.exp2(nt(left, right)))
            main = main + nn(w1, jnp.concatenate([high, low], axis=1))
            rest = rest + nn(w2, high)
    total = main[:, :LANES] + (main[:, LANES:] + rest)
    if not first:
        total = total + total_in[...]
    if last:
        for j in range(CAP):
            total_ref[pl.ds(j, rows, stride=CAP), :] = total[j * rows : (j + 1) * rows, :]
    else:
        total_ref[...] = total


def take_kernel(choose_ref, back_ref, out_ref):
    picked = nn(choose_ref[...], jnp.concatenate(split3(back_ref[...]), axis=1))
    out_ref[...] = picked[:, :LANES] + picked[:, LANES : 2 * LANES] + picked[:, 2 * LANES :]


def coords_kernel(here_ref, out_ref):
    for h in range(CAP // 2):
        out_ref[pl.ds(h * LANES, LANES), :] = here_ref[pl.ds(CAP + h, LANES, stride=UNIT), :]


def whole(count):
    return [pl.BlockSpec(memory_space=pltpu.VMEM)] * count


def call(kernel, args, outs, flops):
    single = len(outs) == 1
    return pl.pallas_call(
        kernel,
        out_shape=outs[0] if single else outs,
        in_specs=whole(len(args)),
        out_specs=whole(1)[0] if single else whole(len(outs)),
        compiler_params=pltpu.CompilerParams(vmem_limit_bytes=24 * 1024 * 1024),
        cost_estimate=pl.CostEstimate(flops=flops, bytes_accessed=1 << 10, transcendentals=0),
    )(*args)


def exchanged(value):
    steps = [(z, k, y) for z in range(NODE_Z) for k in range(NODE_X) for y in range(NODE_Y)]
    order = [(y * NODE_Z + z) * NODE_X + (k ^ (k // 2)) for z, k, y in steps]
    return lax.all_to_all(value, "node", split_axis=0, concat_axis=0, axis_index_groups=[order[::-1]], tiled=True)


def swapped(value, axis, mask):
    pairs = [(source, source ^ mask) for source in range(lax.axis_size(axis))]
    return lax.ppermute(value, axis, pairs)


def per_device(points, probes, leaf):
    n_node = lax.axis_size("node")
    f32 = jnp.float32
    slots = n_node * CAP
    bf16 = jnp.bfloat16
    earlier = call(earlier_kernel, (), (jax.ShapeDtypeStruct((LANES, leaf.shape[0]), bf16),), 1 << 33)
    packed, pos = call(
        pack_kernel,
        (earlier, leaf.reshape(1, -1), points.T, probes),
        (jax.ShapeDtypeStruct((n_node * UNIT, LANES), f32), jax.ShapeDtypeStruct((1, leaf.shape[0]), jnp.int32)),
        1 << 28,
    )
    arrived = exchanged(packed.reshape(n_node, 1, UNIT * LANES))
    here = arrived.reshape(n_node * UNIT, LANES)
    far = swapped(here, "slab", 2)
    coords = call(coords_kernel, (here,), (jax.ShapeDtypeStruct((2 * n_node, LANES), f32),), 1 << 10)
    own = swapped(coords, "node", 1)
    beside = swapped(here, "slab", 1)
    total_shape = jax.ShapeDtypeStruct((slots, LANES), f32)
    flops = 1 << 12
    left, total = call(
        functools.partial(block_kernel, blocks=1, first=True, last=False),
        (own, here),
        (jax.ShapeDtypeStruct((slots, 4 * LANES), jnp.bfloat16), total_shape),
        flops,
    )
    middle = functools.partial(block_kernel, blocks=2, first=False, last=False)
    choose = call(choose_kernel, (pos,), (jax.ShapeDtypeStruct((leaf.shape[0], slots), bf16),), 1 << 12)
    far, total, choose = lax.optimization_barrier((far, total, choose))
    far_beside = swapped(far, "slab", 1)
    total = call(middle, (left, total, far, beside), (total_shape,), flops)
    total = call(
        functools.partial(block_kernel, blocks=1, first=False, last=True), (left, total, far_beside), (total_shape,), flops
    )
    back = exchanged(total.reshape(n_node, CAP, LANES)).reshape(slots, LANES)
    return call(take_kernel, (choose, back), (jax.ShapeDtypeStruct(probes.shape, f32),), 1 << 27)


def solution(mesh):
    placed = (P(("node", "slab"), None), P(("node", "slab"), None), P(("node", "slab"), None))
    return jax.shard_map(
        per_device, mesh=mesh, in_specs=placed, out_specs=P(("node", "slab"), None), check_vma=False
    )
```

```python
import functools
import math

import jax
import jax.numpy as jnp
from jax import lax
from jax.experimental import pallas as pl
from jax.experimental.pallas import tpu as pltpu
from jax.sharding import PartitionSpec as P

kernel_scale = 1.0 / 64.0
log2_scale = kernel_scale * math.log2(math.e)
CAP = 4
UNIT = 6
LANES = 128
NODE_Y, NODE_Z, NODE_X = 8, 4, 4


def split2(value):
    high = value.astype(jnp.bfloat16)
    low = (value - high.astype(jnp.float32)).astype(jnp.bfloat16)
    return high, low


def split3(value):
    high = value.astype(jnp.bfloat16)
    rest = value - high.astype(jnp.float32)
    mid = rest.astype(jnp.bfloat16)
    low = (rest - mid.astype(jnp.float32)).astype(jnp.bfloat16)
    return high, mid, low


def iota(shape, dim):
    return lax.broadcasted_iota(jnp.int32, shape, dim)


def nt(a, b):
    return lax.dot_general(a, b, (((1,), (1,)), ((), ())), preferred_element_type=jnp.float32)


def nn(a, b):
    return jnp.dot(a, b, preferred_element_type=jnp.float32)


def mask_bf16(mask):
    return jnp.where(mask, 1.0, 0.0).astype(jnp.bfloat16)


def choose_kernel(pos_ref, choose_ref):
    n = pos_ref.shape[1]
    wanted = jnp.transpose(jnp.broadcast_to(pos_ref[...].astype(jnp.float32), (LANES, n))).astype(jnp.int32)
    lane = iota((n, LANES), 1)
    for k in range(choose_ref.shape[1] // LANES):
        choose_ref[:, k * LANES : (k + 1) * LANES] = mask_bf16(wanted == lane + k * LANES)


def earlier_kernel(out_ref):
    out_ref[...] = mask_bf16(iota(out_ref.shape, 0) < iota(out_ref.shape, 1))


def place(node):
    x = jnp.bitwise_and(node, NODE_X - 1)
    z = jnp.bitwise_and(node // NODE_X, NODE_Z - 1)
    y = node // (NODE_X * NODE_Z)
    x = jnp.bitwise_xor(x, x // 2)
    y = jnp.bitwise_xor(jnp.bitwise_xor(y, y // 2), y // 4)
    z = jnp.bitwise_xor(z, z // 2)
    rank = (z * NODE_Y + y) * NODE_X + x
    return NODE_X * NODE_Y * NODE_Z - 1 - rank


def pack_kernel(earlier_ref, leaf_ref, xt_ref, w_ref, out_ref, pos_ref):
    n = leaf_ref.shape[1]
    dim = xt_ref.shape[0]
    leaf = leaf_ref[...]
    row = iota((LANES, n), 0)
    own = row == leaf
    before = nn(mask_bf16(own), earlier_ref[...])
    slot = jnp.sum(jnp.where(own, before, 0.0), axis=0, keepdims=True).astype(jnp.int32)
    pos_ref[...] = place(leaf) * CAP + slot
    goal = place(jnp.bitwise_xor(leaf, 1)) * CAP + slot
    choose = [mask_bf16(row * CAP == goal - j) for j in range(CAP)]
    picked = nn(jnp.concatenate(choose, axis=0), jnp.concatenate(split3(w_ref[...]), axis=1))
    picked = picked[:, :LANES] + picked[:, LANES : 2 * LANES] + picked[:, 2 * LANES :]
    for j in range(CAP):
        out_ref[pl.ds(j, LANES, stride=UNIT), :] = picked[j * LANES : (j + 1) * LANES, :]
    empty = jnp.zeros((dim, n), jnp.bfloat16)
    x_parts = []
    for part in split3(xt_ref[...]):
        x_parts.append(jnp.concatenate([part, empty], axis=1))
        x_parts.append(jnp.concatenate([empty, part], axis=1))
    pairs = [jnp.concatenate(choose[2 * h : 2 * h + 2], axis=1) for h in range(CAP // 2)]
    picked = nt(jnp.concatenate(pairs, axis=0), jnp.concatenate(x_parts, axis=0))
    picked = picked[:, :LANES] + picked[:, LANES : 2 * LANES] + picked[:, 2 * LANES :]
    for h in range(CAP // 2):
        out_ref[pl.ds(CAP + h, LANES, stride=UNIT), :] = picked[h * LANES : (h + 1) * LANES, :]


def doubled(pair):
    turned = pltpu.roll(pair, 64, 1)
    low = iota(pair.shape, 1) < 64
    return jnp.concatenate([jnp.where(low, pair, turned), jnp.where(low, turned, pair)], axis=0)


def square_parts(x):
    total = jnp.sum(x * x, axis=1, keepdims=True) * (-0.5 * log2_scale)
    return [part.astype(jnp.float32) for part in split3(jnp.broadcast_to(total, x.shape))]


def left_operand(pair):
    x = doubled(pair)
    lane = iota(x.shape, 1)
    low = lane < 64
    s1, s2, s3 = square_parts(x)
    a1, a2, a3 = [part.astype(jnp.float32) for part in split3(x * (2.0 * log2_scale))]
    tail = jnp.where(lane < 3, 1.0, jnp.where(lane == 3, s1, jnp.where(lane == 4, s2, jnp.where(lane == 5, s3, 0.0))))
    parts = [a1, jnp.where(low, a2, a1), jnp.where(low, a3, a2), tail]
    return jnp.concatenate([part.astype(jnp.bfloat16) for part in parts], axis=1)


def right_operand(pair):
    x = doubled(pair)
    lane = iota(x.shape, 1)
    low = lane < 64
    s1, s2, s3 = square_parts(x)
    x1, x2, x3 = [part.astype(jnp.float32) for part in split3(x)]
    tail = jnp.where(lane == 0, s1, jnp.where(lane == 1, s2, jnp.where(lane == 2, s3, jnp.where(lane < 6, 1.0, 0.0))))
    first = jnp.where(low, x1, x2).astype(jnp.bfloat16)
    parts = [first, jnp.where(low, x1, x3).astype(jnp.bfloat16), first, tail.astype(jnp.bfloat16)]
    return jnp.concatenate(parts, axis=1)


def block_kernel(*refs, blocks, first, last):
    refs = list(refs)
    if first:
        own_ref = refs.pop(0)
    else:
        left_in, total_in = refs.pop(0), refs.pop(0)
    cols_refs, refs = refs[:blocks], refs[blocks:]
    rows = LANES
    if first:
        left_ref, total_ref = refs
        for h in range(CAP // 2):
            left_ref[pl.ds(2 * h * rows, 2 * rows), :] = left_operand(own_ref[pl.ds(h * rows, rows), :])
        source = left_ref
    else:
        (total_ref,) = refs
        source = left_in
    left = source[...]
    main, rest = 0.0, 0.0
    for cols_ref in cols_refs:
        for h in range(CAP // 2):
            right = right_operand(cols_ref[pl.ds(CAP + h, rows, stride=UNIT), :])
            w = jnp.concatenate([cols_ref[pl.ds(2 * h + e, rows, stride=UNIT), :] for e in range(2)], axis=0)
            high, low = split2(w)
            w1, w2 = split2(jnp.exp2(nt(left, right)))
            main = main + nn(w1, jnp.concatenate([high, low], axis=1))
            rest = rest + nn(w2, high)
    total = main[:, :LANES] + (main[:, LANES:] + rest)
    if not first:
        total = total + total_in[...]
    if last:
        for j in range(CAP):
            total_ref[pl.ds(j, rows, stride=CAP), :] = total[j * rows : (j + 1) * rows, :]
    else:
        total_ref[...] = total


def take_kernel(choose_ref, back_ref, out_ref):
    picked = nn(choose_ref[...], jnp.concatenate(split3(back_ref[...]), axis=1))
    out_ref[...] = picked[:, :LANES] + picked[:, LANES : 2 * LANES] + picked[:, 2 * LANES :]


def coords_kernel(here_ref, out_ref):
    for h in range(CAP // 2):
        out_ref[pl.ds(h * LANES, LANES), :] = here_ref[pl.ds(CAP + h, LANES, stride=UNIT), :]


def whole(count):
    return [pl.BlockSpec(memory_space=pltpu.VMEM)] * count


def call(kernel, args, outs, flops):
    single = len(outs) == 1
    return pl.pallas_call(
        kernel,
        out_shape=outs[0] if single else outs,
        in_specs=whole(len(args)),
        out_specs=whole(1)[0] if single else whole(len(outs)),
        compiler_params=pltpu.CompilerParams(vmem_limit_bytes=24 * 1024 * 1024),
        cost_estimate=pl.CostEstimate(flops=flops, bytes_accessed=1 << 10, transcendentals=0),
    )(*args)


def exchanged(value):
    gray = lambda count: [k ^ (k // 2) for k in range(count)]
    order = [(y * NODE_Z + z) * NODE_X + x for z in gray(NODE_Z) for y in gray(NODE_Y) for x in gray(NODE_X)]
    return lax.all_to_all(value, "node", split_axis=0, concat_axis=0, axis_index_groups=[order[::-1]], tiled=True)


def swapped(value, axis, mask):
    pairs = [(source, source ^ mask) for source in range(lax.axis_size(axis))]
    return lax.ppermute(value, axis, pairs)


def per_device(points, probes, leaf):
    n_node = lax.axis_size("node")
    f32 = jnp.float32
    slots = n_node * CAP
    bf16 = jnp.bfloat16
    earlier = call(earlier_kernel, (), (jax.ShapeDtypeStruct((LANES, leaf.shape[0]), bf16),), 1 << 33)
    packed, pos = call(
        pack_kernel,
        (earlier, leaf.reshape(1, -1), points.T, probes),
        (jax.ShapeDtypeStruct((n_node * UNIT, LANES), f32), jax.ShapeDtypeStruct((1, leaf.shape[0]), jnp.int32)),
        1 << 28,
    )
    arrived = exchanged(packed.reshape(n_node, 1, UNIT * LANES))
    here = arrived.reshape(n_node * UNIT, LANES)
    far = swapped(here, "slab", 2)
    coords = call(coords_kernel, (here,), (jax.ShapeDtypeStruct((2 * n_node, LANES), f32),), 1 << 10)
    own = swapped(coords, "node", 1)
    beside = swapped(here, "slab", 1)
    total_shape = jax.ShapeDtypeStruct((slots, LANES), f32)
    flops = 1 << 12
    left, total = call(
        functools.partial(block_kernel, blocks=1, first=True, last=False),
        (own, here),
        (jax.ShapeDtypeStruct((slots, 4 * LANES), jnp.bfloat16), total_shape),
        flops,
    )
    middle = functools.partial(block_kernel, blocks=2, first=False, last=False)
    choose = call(choose_kernel, (pos,), (jax.ShapeDtypeStruct((leaf.shape[0], slots), bf16),), 1 << 12)
    far, total, choose = lax.optimization_barrier((far, total, choose))
    far_beside = swapped(far, "slab", 1)
    total = call(middle, (left, total, far, beside), (total_shape,), flops)
    total = call(
        functools.partial(block_kernel, blocks=1, first=False, last=True), (left, total, far_beside), (total_shape,), flops
    )
    back = exchanged(total.reshape(n_node, CAP, LANES)).reshape(slots, LANES)
    return call(take_kernel, (choose, back), (jax.ShapeDtypeStruct(probes.shape, f32),), 1 << 27)


def solution(mesh):
    placed = (P(("node", "slab"), None), P(("node", "slab"), None), P(("node", "slab"), None))
    return jax.shard_map(
        per_device, mesh=mesh, in_specs=placed, out_specs=P(("node", "slab"), None), check_vma=False
    )
```

```python
import functools
import math

import jax
import jax.numpy as jnp
from jax import lax
from jax.experimental import pallas as pl
from jax.experimental.pallas import tpu as pltpu
from jax.sharding import PartitionSpec as P

kernel_scale = 1.0 / 64.0
log2_scale = kernel_scale * math.log2(math.e)
CAP = 4
UNIT = 6
LANES = 128
NODE_Y, NODE_Z, NODE_X = 8, 4, 4


def split2(value):
    high = value.astype(jnp.bfloat16)
    low = (value - high.astype(jnp.float32)).astype(jnp.bfloat16)
    return high, low


def split3(value):
    high = value.astype(jnp.bfloat16)
    rest = value - high.astype(jnp.float32)
    mid = rest.astype(jnp.bfloat16)
    low = (rest - mid.astype(jnp.float32)).astype(jnp.bfloat16)
    return high, mid, low


def iota(shape, dim):
    return lax.broadcasted_iota(jnp.int32, shape, dim)


def nt(a, b):
    return lax.dot_general(a, b, (((1,), (1,)), ((), ())), preferred_element_type=jnp.float32)


def nn(a, b):
    return jnp.dot(a, b, preferred_element_type=jnp.float32)


def mask_bf16(mask):
    return jnp.where(mask, 1.0, 0.0).astype(jnp.bfloat16)


def choose_kernel(pos_ref, choose_ref):
    n = pos_ref.shape[1]
    wanted = jnp.transpose(jnp.broadcast_to(pos_ref[...].astype(jnp.float32), (LANES, n))).astype(jnp.int32)
    lane = iota((n, LANES), 1)
    for k in range(choose_ref.shape[1] // LANES):
        choose_ref[:, k * LANES : (k + 1) * LANES] = mask_bf16(wanted == lane + k * LANES)


def earlier_kernel(out_ref):
    out_ref[...] = mask_bf16(iota(out_ref.shape, 0) < iota(out_ref.shape, 1))


def place(node):
    x = jnp.bitwise_and(node, NODE_X - 1)
    z = jnp.bitwise_and(node // NODE_X, NODE_Z - 1)
    y = node // (NODE_X * NODE_Z)
    x = jnp.bitwise_xor(x, x // 2)
    y = jnp.bitwise_xor(jnp.bitwise_xor(y, y // 2), y // 4)
    rank = (z * NODE_X + x) * NODE_Y + y
    return NODE_X * NODE_Y * NODE_Z - 1 - rank


def pack_kernel(earlier_ref, leaf_ref, xt_ref, w_ref, out_ref, pos_ref):
    n = leaf_ref.shape[1]
    dim = xt_ref.shape[0]
    leaf = leaf_ref[...]
    row = iota((LANES, n), 0)
    own = row == leaf
    before = nn(mask_bf16(own), earlier_ref[...])
    slot = jnp.sum(jnp.where(own, before, 0.0), axis=0, keepdims=True).astype(jnp.int32)
    pos_ref[...] = place(leaf) * CAP + slot
    goal = place(jnp.bitwise_xor(leaf, 1)) * CAP + slot
    choose = [mask_bf16(row * CAP == goal - j) for j in range(CAP)]
    picked = nn(jnp.concatenate(choose, axis=0), jnp.concatenate(split3(w_ref[...]), axis=1))
    picked = picked[:, :LANES] + picked[:, LANES : 2 * LANES] + picked[:, 2 * LANES :]
    for j in range(CAP):
        out_ref[pl.ds(j, LANES, stride=UNIT), :] = picked[j * LANES : (j + 1) * LANES, :]
    empty = jnp.zeros((dim, n), jnp.bfloat16)
    x_parts = []
    for part in split3(xt_ref[...]):
        x_parts.append(jnp.concatenate([part, empty], axis=1))
        x_parts.append(jnp.concatenate([empty, part], axis=1))
    pairs = [jnp.concatenate(choose[2 * h : 2 * h + 2], axis=1) for h in range(CAP // 2)]
    picked = nt(jnp.concatenate(pairs, axis=0), jnp.concatenate(x_parts, axis=0))
    picked = picked[:, :LANES] + picked[:, LANES : 2 * LANES] + picked[:, 2 * LANES :]
    for h in range(CAP // 2):
        out_ref[pl.ds(CAP + h, LANES, stride=UNIT), :] = picked[h * LANES : (h + 1) * LANES, :]


def doubled(pair):
    turned = pltpu.roll(pair, 64, 1)
    low = iota(pair.shape, 1) < 64
    return jnp.concatenate([jnp.where(low, pair, turned), jnp.where(low, turned, pair)], axis=0)


def square_parts(x):
    total = jnp.sum(x * x, axis=1, keepdims=True) * (-0.5 * log2_scale)
    return [part.astype(jnp.float32) for part in split3(jnp.broadcast_to(total, x.shape))]


def left_operand(pair):
    x = doubled(pair)
    lane = iota(x.shape, 1)
    low = lane < 64
    s1, s2, s3 = square_parts(x)
    a1, a2, a3 = [part.astype(jnp.float32) for part in split3(x * (2.0 * log2_scale))]
    tail = jnp.where(lane < 3, 1.0, jnp.where(lane == 3, s1, jnp.where(lane == 4, s2, jnp.where(lane == 5, s3, 0.0))))
    parts = [a1, jnp.where(low, a2, a1), jnp.where(low, a3, a2), tail]
    return jnp.concatenate([part.astype(jnp.bfloat16) for part in parts], axis=1)


def right_operand(pair):
    x = doubled(pair)
    lane = iota(x.shape, 1)
    low = lane < 64
    s1, s2, s3 = square_parts(x)
    x1, x2, x3 = [part.astype(jnp.float32) for part in split3(x)]
    tail = jnp.where(lane == 0, s1, jnp.where(lane == 1, s2, jnp.where(lane == 2, s3, jnp.where(lane < 6, 1.0, 0.0))))
    first = jnp.where(low, x1, x2).astype(jnp.bfloat16)
    parts = [first, jnp.where(low, x1, x3).astype(jnp.bfloat16), first, tail.astype(jnp.bfloat16)]
    return jnp.concatenate(parts, axis=1)


def block_kernel(*refs, blocks, first, last):
    refs = list(refs)
    if first:
        own_ref = refs.pop(0)
    else:
        left_in, total_in = refs.pop(0), refs.pop(0)
    cols_refs, refs = refs[:blocks], refs[blocks:]
    rows = LANES
    if first:
        left_ref, total_ref = refs
        for h in range(CAP // 2):
            left_ref[pl.ds(2 * h * rows, 2 * rows), :] = left_operand(own_ref[pl.ds(h * rows, rows), :])
        source = left_ref
    else:
        (total_ref,) = refs
        source = left_in
    left = source[...]
    main, rest = 0.0, 0.0
    for cols_ref in cols_refs:
        for h in range(CAP // 2):
            right = right_operand(cols_ref[pl.ds(CAP + h, rows, stride=UNIT), :])
            w = jnp.concatenate([cols_ref[pl.ds(2 * h + e, rows, stride=UNIT), :] for e in range(2)], axis=0)
            high, low = split2(w)
            w1, w2 = split2(jnp.exp2(nt(left, right)))
            main = main + nn(w1, jnp.concatenate([high, low], axis=1))
            rest = rest + nn(w2, high)
    total = main[:, :LANES] + (main[:, LANES:] + rest)
    if not first:
        total = total + total_in[...]
    if last:
        for j in range(CAP):
            total_ref[pl.ds(j, rows, stride=CAP), :] = total[j * rows : (j + 1) * rows, :]
    else:
        total_ref[...] = total


def take_kernel(choose_ref, back_ref, out_ref):
    picked = nn(choose_ref[...], jnp.concatenate(split3(back_ref[...]), axis=1))
    out_ref[...] = picked[:, :LANES] + picked[:, LANES : 2 * LANES] + picked[:, 2 * LANES :]


def coords_kernel(here_ref, out_ref):
    for h in range(CAP // 2):
        out_ref[pl.ds(h * LANES, LANES), :] = here_ref[pl.ds(CAP + h, LANES, stride=UNIT), :]


def whole(count):
    return [pl.BlockSpec(memory_space=pltpu.VMEM)] * count


def call(kernel, args, outs, flops):
    single = len(outs) == 1
    return pl.pallas_call(
        kernel,
        out_shape=outs[0] if single else outs,
        in_specs=whole(len(args)),
        out_specs=whole(1)[0] if single else whole(len(outs)),
        compiler_params=pltpu.CompilerParams(vmem_limit_bytes=24 * 1024 * 1024),
        cost_estimate=pl.CostEstimate(flops=flops, bytes_accessed=1 << 10, transcendentals=0),
    )(*args)


def exchanged(value):
    gray = lambda count: [k ^ (k // 2) for k in range(count)]
    order = [(y * NODE_Z + z) * NODE_X + x for z in range(NODE_Z) for x in gray(NODE_X) for y in gray(NODE_Y)]
    return lax.all_to_all(value, "node", split_axis=0, concat_axis=0, axis_index_groups=[order[::-1]], tiled=True)


def swapped(value, axis, mask):
    pairs = [(source, source ^ mask) for source in range(lax.axis_size(axis))]
    return lax.ppermute(value, axis, pairs)


def per_device(points, probes, leaf):
    n_node = lax.axis_size("node")
    f32 = jnp.float32
    slots = n_node * CAP
    bf16 = jnp.bfloat16
    earlier = call(earlier_kernel, (), (jax.ShapeDtypeStruct((LANES, leaf.shape[0]), bf16),), 1 << 33)
    packed, pos = call(
        pack_kernel,
        (earlier, leaf.reshape(1, -1), points.T, probes),
        (jax.ShapeDtypeStruct((n_node * UNIT, LANES), f32), jax.ShapeDtypeStruct((1, leaf.shape[0]), jnp.int32)),
        1 << 28,
    )
    arrived = exchanged(packed.reshape(n_node, 1, UNIT * LANES))
    here = arrived.reshape(n_node * UNIT, LANES)
    far = swapped(here, "slab", 2)
    coords = call(coords_kernel, (here,), (jax.ShapeDtypeStruct((2 * n_node, LANES), f32),), 1 << 10)
    own = swapped(coords, "node", 1)
    beside = swapped(here, "slab", 1)
    total_shape = jax.ShapeDtypeStruct((slots, LANES), f32)
    flops = 1 << 12
    left, total = call(
        functools.partial(block_kernel, blocks=1, first=True, last=False),
        (own, here),
        (jax.ShapeDtypeStruct((slots, 4 * LANES), jnp.bfloat16), total_shape),
        flops,
    )
    middle = functools.partial(block_kernel, blocks=2, first=False, last=False)
    choose = call(choose_kernel, (pos,), (jax.ShapeDtypeStruct((leaf.shape[0], slots), bf16),), 1 << 12)
    far, total, choose = lax.optimization_barrier((far, total, choose))
    far_beside = swapped(far, "slab", 1)
    total = call(middle, (left, total, far, beside), (total_shape,), flops)
    total = call(
        functools.partial(block_kernel, blocks=1, first=False, last=True), (left, total, far_beside), (total_shape,), flops
    )
    back = exchanged(total.reshape(n_node, CAP, LANES)).reshape(slots, LANES)
    return call(take_kernel, (choose, back), (jax.ShapeDtypeStruct(probes.shape, f32),), 1 << 27)


def solution(mesh):
    placed = (P(("node", "slab"), None), P(("node", "slab"), None), P(("node", "slab"), None))
    return jax.shard_map(
        per_device, mesh=mesh, in_specs=placed, out_specs=P(("node", "slab"), None), check_vma=False
    )
```
